512 devices in a mesh: dom: 64 (over z, y), feat: 8 (over x, core).
Axes of the slice: x: 4, y: 8, z: 8, core: 2. Of those that a mesh axis runs over, the one named last changes fastest.
Arguments:
- features: bfloat16 [256, 49152], P('feat', 'dom'), may hold values from -6 to 6
- weight: bfloat16 [256, 256], replicated, may hold values from -0.375 to 0.375
- cotangent: bfloat16 [256, 49152], P('feat', 'dom'), may hold values from -6 to 6
- tile_vals: bfloat16 [4480, 128, 128], P('dom'), may hold values from -0.375 to 0.375
- tile_src: int32 [4480], P('dom'), may hold values from 0 to 69, as said below
- tile_dst: int32 [4480], P('dom'), may hold values from 0 to 5
- tile_count: int32 [64], P('dom'), may hold values from 6 to 70, as said below
- halo_block: int32 [64, 64], P('dom'), may hold values from -1 to 5, as said below
Outputs:
- activated: bfloat16 [256, 49152], P('feat', 'dom')
- feature_grad: bfloat16 [256, 49152], P('feat', 'dom')
- weight_grad: float32 [256, 256], P('feat')
The draws below stay inside these ranges and needn't reach their ends.
Inputs may be any that keep to these rules, and one draw needn't show every extreme that they name: halo_block[p, q] is a block index of partition q or -1 (p reads nothing of q); halo_block[p, p] = -1. Partition p's valid tiles are its first tile_count[p] tile slots; tile_count[p] is at least 6 plus the number of q with halo_block[p, q] >= 0. Every tile of partition p has tile_src below 6, or tile_src = 6 + q with halo_block[p, q] >= 0. Among p's valid tiles each of its own blocks and each q with halo_block[p, q] >= 0 is named at least once.
All inputs are finite; a program needn't handle non-finite values.
Results may differ from the reference program's by a relative error of at most 0.0064.
Values may be sent and summed in bfloat16 or wider, within the bound.
No kernel may reach another device: no remote copies, remote signals or barrier semaphores. Data moves between devices by JAX's collectives and lax.ppermute only.
A program may use at most 64 MiB of HBM per device.

```python
import math
import jax
import jax.numpy as jnp
from jax import lax

F = 256
BS = 128
BLK_DEV = 6
PARTITIONS = 64
TILES = 70
NODES = 49152


def graph_layout(key):
    key = jax.random.fold_in(key, 11)
    pick_keys = jax.random.split(key, 3)
    forced_halo = jax.random.randint(pick_keys[0], (), 0, PARTITIONS)
    forced_full = jax.random.randint(pick_keys[1], (), 0, PARTITIONS)

    def one_partition(index):
        part_key = jax.random.fold_in(pick_keys[2], index)
        keys = jax.random.split(part_key, 6)
        owners = jnp.arange(PARTITIONS, dtype=jnp.int32)
        density = jax.random.randint(keys[0], (), 1, 5)
        live = (jax.random.randint(keys[1], (PARTITIONS,), 0, 4) < density) & (owners != index)
        forced_peer = (index + 1) % PARTITIONS
        forcing = (index == forced_halo) & (owners == forced_peer) & (forced_peer != index)
        live = live | forcing
        chosen = jax.random.randint(keys[2], (PARTITIONS,), 0, BLK_DEV)
        chosen = jnp.where(forcing, BLK_DEV - 1, chosen)
        halo = jnp.where(live, chosen, -1).astype(jnp.int32)
        live_count = jnp.sum(live.astype(jnp.int32))
        surplus = jax.random.randint(keys[3], (), BLK_DEV, TILES - live_count + 1)
        valid_count = jnp.where(index == forced_full, TILES, live_count + surplus).astype(jnp.int32)
        order = jnp.argsort(jnp.where(live, owners, PARTITIONS + owners), stable=True).astype(jnp.int32)
        slots = jnp.arange(TILES, dtype=jnp.int32)
        halo_pos = jnp.clip(slots, 0, PARTITIONS - 1)
        local_pos = jnp.clip(slots - live_count, 0, BLK_DEV - 1)
        listed = jnp.where(slots < live_count, BLK_DEV + order[halo_pos], local_pos)
        covered = live_count + BLK_DEV
        repeats = jax.random.randint(keys[4], (TILES,), 0, covered)
        listed = jnp.where(slots < covered, listed, listed[repeats])
        scores = jax.random.randint(keys[5], (TILES,), 0, 1 << 16) * TILES + slots
        scores = jnp.where(slots < valid_count, scores, (1 << 28) + slots)
        shuffle = jnp.argsort(scores, stable=True)
        sources = listed[shuffle].astype(jnp.int32)
        return (halo, valid_count, sources)
    return jax.vmap(one_partition)(jnp.arange(PARTITIONS, dtype=jnp.int32))


def draw_halo_block(key, part):
    layout = graph_layout(key)
    return layout[0]


def draw_tile_count(key, part):
    layout = graph_layout(key)
    return layout[1]


def draw_tile_src(key, part):
    layout = graph_layout(key)
    return layout[2].reshape(-1)


def with_ends(values, rng, smallest, largest):
    longest = values.shape.index(max(values.shape))
    spots = []
    for shift in (0, 1):
        where = [jax.random.randint(jax.random.fold_in(rng, axis), (), 0, length) for axis, length in enumerate(values.shape)]
        where[longest] = (where[longest] + shift) % values.shape[longest]
        spots.append(tuple(where))
    return values.at[spots[0]].set(smallest).at[spots[1]].set(largest)


def block_levels(stream_key, dims, shards, least, largest):
    def one(position, parts):
        heights = jax.random.uniform(jax.random.fold_in(jax.random.fold_in(stream_key, 6), position), (parts,), jnp.float32, least / len(shards), largest / len(shards))
        return jnp.repeat(jnp.exp(heights), dims[position] // parts).reshape((-1,) + (1,) * (len(dims) - position - 1))

    loudness = one(*shards[0])
    for cut in shards[1:]:
        loudness = loudness * one(*cut)
    return loudness


def bell_draw(own_key, shape, spread, most, cuts=(), held_as=jnp.bfloat16):
    loudness = block_levels(own_key, shape, cuts, -0.22, 0.18) if cuts else 1.0
    array = jax.random.normal(own_key, shape, jnp.float32) * spread * loudness
    return jnp.minimum(jnp.maximum(array, -most), most).astype(held_as)


def setup_inputs(seed: int = 0) -> dict:
    streams_of = jax.random.split(jax.random.key(seed), 9)
    return {
        "features": bell_draw(streams_of[0], (F, NODES), 1.0, 6.0, ((0, 8), (1, 64))),
        "weight": bell_draw(streams_of[1], (F, F), F ** -0.5, 0.375),
        "cotangent": bell_draw(streams_of[2], (F, NODES), 1.0, 6.0, ((0, 8), (1, 64))),
        "tile_vals": bell_draw(streams_of[3], (PARTITIONS * TILES, BS, BS), (2 * BS) ** -0.5, 0.375, ((0, 64),)),
        "tile_src": draw_tile_src(jax.random.fold_in(streams_of[8], 71), 0),
        "tile_dst": with_ends(jax.random.randint(streams_of[5], (PARTITIONS * TILES,), 0, BLK_DEV), jax.random.fold_in(streams_of[5], 1), 0, BLK_DEV - 1).astype(jnp.int32),
        "tile_count": draw_tile_count(jax.random.fold_in(streams_of[8], 71), 0),
        "halo_block": draw_halo_block(jax.random.fold_in(streams_of[8], 71), 0),
    }


HIGHEST = lax.Precision.HIGHEST

def reference(features, weight, cotangent, tile_vals, tile_src, tile_dst, tile_count, halo_block):
    feat_blocks = features.reshape(F, PARTITIONS, BLK_DEV, BS).transpose(1, 2, 0, 3)
    tile_table = tile_vals.reshape(PARTITIONS, TILES, BS, BS)
    src_lists = tile_src.reshape(PARTITIONS, TILES)
    dst_lists = tile_dst.reshape(PARTITIONS, TILES)
    owners = jnp.arange(PARTITIONS, dtype=jnp.int32)
    slots = jnp.arange(TILES, dtype=jnp.int32)
    local_ids = jnp.arange(BLK_DEV, dtype=jnp.int32)
    source_ids = jnp.arange(BLK_DEV + PARTITIONS, dtype=jnp.int32)

    def forward_part(index):
        wanted = halo_block[index]
        halo = feat_blocks[owners, jnp.clip(wanted, 0, BLK_DEV - 1)]
        halo = jnp.where((wanted >= 0)[:, None, None], halo, jnp.zeros((), features.dtype))
        source = jnp.concatenate([feat_blocks[index], halo], axis=0)
        picked = source[src_lists[index]].astype(jnp.float32)
        tile_terms = jnp.einsum('tfj,tij->tfi', picked, tile_table[index].astype(jnp.float32))
        live_tile = (slots < tile_count[index]).astype(jnp.float32)
        dst_table = (dst_lists[index][None, :] == local_ids[:, None]).astype(jnp.float32) * live_tile[None, :]
        return jnp.einsum('dt,tfi->dfi', dst_table, tile_terms, precision=HIGHEST).astype(jnp.bfloat16)
    agg_parts = lax.map(forward_part, owners)
    aggregated = agg_parts.transpose(2, 0, 1, 3).reshape(F, NODES)
    preact = jnp.dot(weight.T, aggregated, preferred_element_type=jnp.float32)
    activated = jax.nn.silu(preact).astype(jnp.bfloat16)
    sigmoid_pre = jax.nn.sigmoid(preact)
    pre_grad = (cotangent.astype(jnp.float32) * sigmoid_pre * (1.0 + preact * (1.0 - sigmoid_pre))).astype(jnp.bfloat16)
    weight_grad = jnp.dot(aggregated, pre_grad.T, preferred_element_type=jnp.float32) * (1.0 / math.sqrt(NODES))
    agg_grad = jnp.dot(weight, pre_grad, preferred_element_type=jnp.float32).astype(jnp.bfloat16)
    grad_blocks = agg_grad.reshape(F, PARTITIONS, BLK_DEV, BS).transpose(1, 2, 0, 3)

    def backward_part(running, index):
        at_dst = grad_blocks[index][dst_lists[index]].astype(jnp.float32)
        back_terms = jnp.einsum('tfi,tij->tfj', at_dst, tile_table[index].astype(jnp.float32))
        live_tile = (slots < tile_count[index]).astype(jnp.float32)
        src_table = (src_lists[index][None, :] == source_ids[:, None]).astype(jnp.float32) * live_tile[None, :]
        src_sums = jnp.einsum('st,tfj->sfj', src_table, back_terms, precision=HIGHEST)
        running = running.at[index].add(src_sums[:BLK_DEV])
        wanted = halo_block[index]
        halo_terms = jnp.where((wanted >= 0)[:, None, None], src_sums[BLK_DEV:], jnp.zeros((), jnp.float32))
        running = running.at[owners, jnp.clip(wanted, 0, BLK_DEV - 1)].add(halo_terms)
        return (running, None)
    running, _ = lax.scan(backward_part, jnp.zeros((PARTITIONS, BLK_DEV, F, BS), jnp.float32), owners)
    feature_grad = running.transpose(2, 0, 1, 3).reshape(F, NODES).astype(jnp.bfloat16)
    return (activated, feature_grad, weight_grad)
```

```python
import functools
import math

import jax
import jax.numpy as jnp
from jax import lax
from jax.experimental import pallas as pl
from jax.experimental.pallas import tpu as pltpu
from jax.sharding import PartitionSpec as P

BF16, F32 = jnp.bfloat16, jnp.float32
SMEM = pl.BlockSpec(memory_space=pltpu.SMEM)
VMEM = pl.BlockSpec(memory_space=pltpu.VMEM)
CHUNK = 10
EXTRA = 16


def call(kernel, out_shape, in_specs, out_specs=None, scratch=(), flops=1000, nbytes=1000, aliases=None):
    return pl.pallas_call(
        kernel,
        out_shape=out_shape,
        in_specs=in_specs,
        out_specs=VMEM if out_specs is None else out_specs,
        scratch_shapes=list(scratch),
        input_output_aliases=aliases or {},
        cost_estimate=pl.CostEstimate(flops=flops, bytes_accessed=nbytes, transcendentals=0),
        compiler_params=pltpu.CompilerParams(vmem_limit_bytes=24 * 1024 * 1024),
    )


def request_kernel(halo_ref, out_ref):
    for q in range(out_ref.shape[0]):
        out_ref[q] = jnp.full((1, out_ref.shape[2]), halo_ref[0, q], jnp.int32)


def pack_kernel(asked_ref, feat_ref, out_ref):
    peers, _, lanes = out_ref.shape
    blocks = feat_ref.shape[1] // lanes
    own = [feat_ref[:, b * lanes : (b + 1) * lanes].astype(F32) for b in range(blocks)]
    for q in range(peers):
        want = jnp.broadcast_to(asked_ref[q], own[0].shape)
        piece = own[0]
        for b in range(1, blocks):
            piece = jnp.where(want == b, own[b], piece)
        out_ref[q] = piece.astype(BF16)


def forward_kernel(src_ref, dst_ref, count_ref, feat_ref, halo_ref, tiles_ref, out_ref, acc_ref):
    tile_total, lanes, _ = tiles_ref.shape
    blocks = feat_ref.shape[1] // lanes
    count = count_ref[0]
    acc_ref[...] = jnp.zeros_like(acc_ref)

    def chunk(c):
        terms = []
        for i in range(CHUNK):
            t = c * CHUNK + i
            src = src_ref[t]
            start = pl.multiple_of(jnp.minimum(src, blocks - 1) * lanes, lanes)
            own = feat_ref[:, pl.ds(start, lanes)]
            far = halo_ref[jnp.maximum(src - blocks, 0)]
            picked = jnp.where(src < blocks, own, far)
            term = lax.dot_general(
                picked, tiles_ref[t], (((1,), (1,)), ((), ())), preferred_element_type=F32
            )
            terms.append(jnp.where(t < count, term, 0.0))
        for i in range(CHUNK):
            acc_ref[dst_ref[c * CHUNK + i]] += terms[i]

    @pl.loop(0, tile_total // CHUNK)
    def _(c):
        @pl.when(c * CHUNK < count)
        def _():
            chunk(c)

    for b in range(blocks):
        block = acc_ref[b].astype(BF16)
        for e in range(out_ref.shape[0]):
            out_ref[e, :, b * lanes : (b + 1) * lanes] = block


def middle_kernel(index_ref, agg_ref, weight_t_ref, cot_ref, pre_ref, part_ref):
    feats, rows, nodes = agg_ref.shape
    agg = agg_ref[...].reshape(feats * rows, nodes)
    pre = jnp.dot(weight_t_ref[...], agg, preferred_element_type=F32)
    sig = jax.nn.sigmoid(pre)
    grad = (cot_ref[...].astype(F32) * sig * (1.0 + pre * (1.0 - sig))).astype(BF16)
    pre_ref[...] = grad
    part = lax.dot_general(
        agg_ref[index_ref[0]], grad, (((1,), (1,)), ((), ())), preferred_element_type=F32
    )
    part_ref[...] = part.reshape(part_ref.shape)


def backward_kernel(
    index_ref, src_ref, dst_ref, count_ref, pre_ref, weight_ref, weight_t_ref, agg_ref, tiles_ref,
    out_ref, own_ref, act_ref, acc_ref, grad_ref,
):
    feats, rows, nodes = agg_ref.shape
    tile_total, lanes, _ = tiles_ref.shape
    blocks = nodes // lanes
    count = count_ref[0]
    mine = pl.ds(pl.multiple_of(index_ref[0] * rows, rows), rows)
    grad_ref[...] = jnp.dot(weight_ref[mine, :], pre_ref[...], preferred_element_type=F32).astype(BF16)
    acc_ref[...] = jnp.zeros_like(acc_ref)

    def chunk(c):
        terms = []
        for i in range(CHUNK):
            t = c * CHUNK + i
            start = pl.multiple_of(dst_ref[t] * lanes, lanes)
            term = jnp.dot(grad_ref[:, pl.ds(start, lanes)], tiles_ref[t], preferred_element_type=F32)
            terms.append(jnp.where(t < count, term, 0.0))
        for i in range(CHUNK):
            acc_ref[src_ref[c * CHUNK + i]] += terms[i]

    @pl.loop(0, tile_total // CHUNK)
    def _(c):
        @pl.when(c * CHUNK < count)
        def _():
            chunk(c)

    own_ref[...] = acc_ref[:blocks]
    for q in range(out_ref.shape[0]):
        out_ref[q, :rows, :] = acc_ref[blocks + q].astype(BF16)
    pre = jnp.dot(
        weight_t_ref[mine, :], agg_ref[...].reshape(feats * rows, nodes), preferred_element_type=F32
    )
    act_ref[...] = jax.nn.silu(pre).astype(BF16)


def attach_kernel(parts_ref, _, out_ref):
    rows = out_ref.shape[1] - EXTRA
    lanes = out_ref.shape[2]
    total = parts_ref[0]
    for i in range(1, parts_ref.shape[0]):
        total = total + parts_ref[i]
    total = total.astype(BF16)
    packed = jnp.concatenate(
        [total[:, i * lanes : (i + 1) * lanes] for i in range(total.shape[1] // lanes)], axis=0
    )
    for q in range(out_ref.shape[0]):
        out_ref[q, rows:, :] = packed


def final_kernel(scale, asked_ref, own_ref, back_ref, grad_ref, weight_ref):
    blocks, rows, lanes = own_ref.shape
    peers = back_ref.shape[0]
    sums = [own_ref[b] for b in range(blocks)]
    pieces = [None] * 4
    for q in range(peers):
        want = jnp.broadcast_to(asked_ref[q], (rows, lanes))
        term = back_ref[q, :rows, :].astype(F32)
        for b in range(blocks):
            sums[b] = sums[b] + jnp.where(want == b, term, 0.0)
        r = (q // 8 % 2) * 2 + q % 2
        piece = back_ref[q, rows:, :].astype(F32)
        pieces[r] = piece if pieces[r] is None else pieces[r] + piece
    for b in range(blocks):
        grad_ref[:, b * lanes : (b + 1) * lanes] = sums[b].astype(BF16)
    for r in range(4):
        height = rows // 4
        for i in range(EXTRA // height):
            weight_ref[r * height : (r + 1) * height, i * lanes : (i + 1) * lanes] = (
                pieces[r][i * height : (i + 1) * height] * scale
            )


def shards(features, weight, cotangent, tile_vals, tile_src, tile_dst, tile_count, halo_block):
    rows, nodes = features.shape
    tiles, lanes, _ = tile_vals.shape
    blocks = nodes // lanes
    peers = lax.axis_size("dom")
    feats = lax.axis_size("feat")
    full = rows * feats
    index = lax.axis_index("feat").reshape(1).astype(jnp.int32)
    shape = jax.ShapeDtypeStruct
    swap = functools.partial(lax.all_to_all, split_axis=0, concat_axis=0, tiled=True)

    request = call(request_kernel, shape((peers, 1, lanes), jnp.int32), [SMEM])(halo_block)
    asked = swap(request, "dom")
    outgoing = call(pack_kernel, shape((peers, rows, lanes), BF16), [VMEM, VMEM])(asked, features)
    incoming = swap(outgoing, "dom")
    cotangent, _ = lax.optimization_barrier((cotangent, asked))
    cot_full = lax.all_gather(cotangent, "feat", axis=0, tiled=True)
    weight_t = weight.T

    spread = call(
        forward_kernel,
        shape((feats, rows, nodes), BF16),
        [SMEM, SMEM, SMEM, VMEM, VMEM, VMEM],
        scratch=[pltpu.VMEM((blocks, rows, lanes), F32)],
    )(tile_src, tile_dst, tile_count, features, incoming, tile_vals)
    agg = swap(spread, "feat")

    pre_grad, part = call(
        middle_kernel,
        (shape((full, nodes), BF16), shape((4, rows // 4, full), F32)),
        [SMEM, VMEM, VMEM, VMEM],
        (VMEM, VMEM),
    )(index, agg, weight_t, cot_full)

    squares = [
        [(2 * a + i) * 8 + 2 * b + j for i in range(2) for j in range(2)]
        for a in range(peers // 16)
        for b in range(4)
    ]
    parts = swap(part, "dom", axis_index_groups=squares)

    outbound, own, activated = call(
        backward_kernel,
        (
            shape((peers, rows + EXTRA, lanes), BF16),
            shape((blocks, rows, lanes), F32),
            shape((rows, nodes), BF16),
        ),
        [SMEM, SMEM, SMEM, SMEM, VMEM, VMEM, VMEM, VMEM, VMEM],
        (VMEM, VMEM, VMEM),
        scratch=[pltpu.VMEM((blocks + peers, rows, lanes), F32), pltpu.VMEM((rows, nodes), BF16)],
        flops=200_000_000,
        nbytes=20_000_000,
    )(index, tile_src, tile_dst, tile_count, pre_grad, weight, weight_t, agg, tile_vals)
    outbound = call(
        attach_kernel, shape((peers, rows + EXTRA, lanes), BF16), [VMEM, VMEM], aliases={1: 0}
    )(parts, outbound)
    returned = swap(outbound, "dom")

    feature_grad, weight_grad = call(
        functools.partial(final_kernel, 1.0 / math.sqrt(peers * nodes)),
        (shape((rows, nodes), BF16), shape((rows, full), F32)),
        [VMEM, VMEM, VMEM],
        (VMEM, VMEM),
    )(asked, own, returned)
    return (activated, feature_grad, weight_grad)


def solution(mesh):
    return jax.shard_map(
        shards,
        mesh=mesh,
        in_specs=(
            P("feat", "dom"),
            P(),
            P("feat", "dom"),
            P("dom", None, None),
            P("dom"),
            P("dom"),
            P("dom"),
            P("dom", None),
        ),
        out_specs=(P("feat", "dom"), P("feat", "dom"), P("feat", None)),
        check_vma=False,
    )
```

```python
import functools
import math

import jax
import jax.numpy as jnp
from jax import lax
from jax.experimental import pallas as pl
from jax.experimental.pallas import tpu as pltpu
from jax.sharding import PartitionSpec as P

BF16, F32 = jnp.bfloat16, jnp.float32
VMEM = pl.BlockSpec(memory_space=pltpu.VMEM)
HBM = pl.BlockSpec(memory_space=pltpu.HBM)
ANY = pl.BlockSpec(memory_space=pl.ANY)
CHUNK = 10
GROUP = 8
EXTRA = 8


def call(kernel, out_shape, in_specs, out_specs=None, scratch=(), flops=1000, nbytes=1000, aliases=None):
    return pl.pallas_call(
        kernel,
        out_shape=out_shape,
        in_specs=in_specs,
        out_specs=VMEM if out_specs is None else out_specs,
        scratch_shapes=list(scratch),
        input_output_aliases=aliases or {},
        cost_estimate=pl.CostEstimate(flops=flops, bytes_accessed=nbytes, transcendentals=0),
        compiler_params=pltpu.CompilerParams(vmem_limit_bytes=24 * 1024 * 1024),
    )


def request_kernel(halo_hbm, feat_hbm, out_ref, feat_ref, halo_ref, sems):
    first = pltpu.make_async_copy(halo_hbm, halo_ref, sems.at[0])
    second = pltpu.make_async_copy(feat_hbm, feat_ref, sems.at[1])
    first.start()
    second.start()
    first.wait()
    for q in range(out_ref.shape[0]):
        out_ref[q] = jnp.full((1, out_ref.shape[2]), halo_ref[0, q], jnp.int32)
    second.wait()


def pack_kernel(asked_ref, feat_ref, out_ref):
    peers, rows, lanes = out_ref.shape
    blocks = feat_ref.shape[1] // lanes
    own = [
        feat_ref[:, b * lanes : (b + 1) * lanes].astype(F32).reshape(rows // 8, 8, lanes)
        for b in range(blocks)
    ]
    for q in range(peers):
        want = jnp.broadcast_to(asked_ref[q], (8, lanes))
        piece = own[0]
        for b in range(1, blocks):
            piece = jnp.where((want == b)[None], own[b], piece)
        out_ref[q] = piece.reshape(rows, lanes).astype(BF16)


def tile_copies(tiles_hbm, tiles_ref, sems):
    return [
        pltpu.make_async_copy(
            tiles_hbm.at[pl.ds(c * CHUNK, CHUNK)], tiles_ref.at[pl.ds(c * CHUNK, CHUNK)], sems.at[c]
        )
        for c in range(tiles_ref.shape[0] // CHUNK)
    ]


def forward_kernel(
    src_hbm, dst_hbm, count_hbm, feat_hbm, halo_ref, tiles_hbm, _,
    out_ref, acc_ref, tiles_ref, feat_ref, src_ref, dst_ref, count_ref, small_sems, sems,
):
    tile_total, lanes, _ = tiles_ref.shape
    blocks = feat_ref.shape[1] // lanes
    small = [
        pltpu.make_async_copy(a, b, small_sems.at[i])
        for i, (a, b) in enumerate(
            ((src_hbm, src_ref), (dst_hbm, dst_ref), (count_hbm, count_ref), (feat_hbm, feat_ref))
        )
    ]
    big = tile_copies(tiles_hbm, tiles_ref, sems)
    for copy in small + big:
        copy.start()
    acc_ref[...] = jnp.zeros_like(acc_ref)
    for copy in small:
        copy.wait()
    count = count_ref[0]

    def chunk(c):
        terms = []
        for i in range(CHUNK):
            t = c * CHUNK + i
            src = src_ref[t]
            start = pl.multiple_of(jnp.minimum(src, blocks - 1) * lanes, lanes)
            own = feat_ref[:, pl.ds(start, lanes)]
            far = halo_ref[jnp.maximum(src - blocks, 0)]
            picked = jnp.where(src < blocks, own, far)
            term = lax.dot_general(
                picked, tiles_ref[t], (((1,), (1,)), ((), ())), preferred_element_type=F32
            )
            terms.append(jnp.where(t < count, term, 0.0))
        for i in range(CHUNK):
            acc_ref[dst_ref[c * CHUNK + i]] += terms[i]

    for c in range(tile_total // CHUNK):
        big[c].wait()
        pl.when(c * CHUNK < count)(functools.partial(chunk, c))

    for b in range(blocks):
        block = acc_ref[b].astype(BF16)
        for e in range(out_ref.shape[0]):
            out_ref[e, :, b * lanes : (b + 1) * lanes] = block


def middle_kernel(agg_ref, weight_ref, weight_t_ref, cot_ref, part_ref, grad_ref, act_ref):
    feats, rows, nodes = agg_ref.shape
    lanes = part_ref.shape[2]
    index = lax.axis_index("feat")
    mine = pl.ds(pl.multiple_of(index * rows, rows), rows)
    agg = agg_ref[...].reshape(feats * rows, nodes)
    pre = jnp.dot(weight_t_ref[...], agg, preferred_element_type=F32)
    sig = jax.nn.sigmoid(pre)
    grad = (cot_ref[...].astype(F32) * sig * (1.0 + pre * (1.0 - sig))).astype(BF16)
    part = lax.dot_general(
        agg_ref[index], grad, (((1,), (1,)), ((), ())), preferred_element_type=F32
    )
    height = rows // GROUP
    for r in range(GROUP):
        part_ref[r] = jnp.concatenate(
            [
                part[r * height : (r + 1) * height, i * lanes : (i + 1) * lanes]
                for i in range(part.shape[1] // lanes)
            ],
            axis=0,
        )
    grad_ref[...] = jnp.dot(weight_ref[mine, :], grad, preferred_element_type=F32).astype(BF16)
    pre_mine = jnp.dot(weight_t_ref[mine, :], agg, preferred_element_type=F32)
    act_ref[...] = jax.nn.silu(pre_mine).astype(BF16)


def backward_kernel(
    src_hbm, dst_hbm, count_hbm, grad_ref, tiles_hbm,
    out_ref, own_hbm, acc_ref, tiles_ref, src_ref, dst_ref, count_ref, small_sems, sems,
):
    rows = grad_ref.shape[0]
    tile_total, lanes, _ = tiles_ref.shape
    blocks = grad_ref.shape[1] // lanes
    small = [
        pltpu.make_async_copy(a, b, small_sems.at[i])
        for i, (a, b) in enumerate(((src_hbm, src_ref), (dst_hbm, dst_ref), (count_hbm, count_ref)))
    ]
    big = tile_copies(tiles_hbm, tiles_ref, sems)
    for copy in small + big:
        copy.start()
    acc_ref[...] = jnp.zeros_like(acc_ref)
    for copy in small:
        copy.wait()
    count = count_ref[0]

    def chunk(c):
        terms = []
        for i in range(CHUNK):
            t = c * CHUNK + i
            start = pl.multiple_of(dst_ref[t] * lanes, lanes)
            term = jnp.dot(grad_ref[:, pl.ds(start, lanes)], tiles_ref[t], preferred_element_type=F32)
            terms.append(jnp.where(t < count, term, 0.0))
        for i in range(CHUNK):
            acc_ref[src_ref[c * CHUNK + i]] += terms[i]

    for c in range(tile_total // CHUNK):
        big[c].wait()
        pl.when(c * CHUNK < count)(functools.partial(chunk, c))

    keep = pltpu.make_async_copy(acc_ref.at[pl.ds(0, blocks)], own_hbm, small_sems.at[3])
    keep.start()
    for q in range(out_ref.shape[0]):
        out_ref[q, :rows, :] = acc_ref[blocks + q].astype(BF16)
    keep.wait()


def attach_kernel(parts_ref, _, out_ref):
    rows = out_ref.shape[1] - EXTRA
    total = parts_ref[0]
    for i in range(1, parts_ref.shape[0]):
        total = total + parts_ref[i]
    total = total.astype(BF16)
    for q in range(out_ref.shape[0]):
        out_ref[q, rows:, :] = total


def final_kernel(scale, asked_ref, own_hbm, back_ref, grad_ref, weight_ref, own_ref, sem):
    blocks, rows, lanes = own_ref.shape
    peers = back_ref.shape[0]
    fetch = pltpu.make_async_copy(own_hbm, own_ref, sem)
    fetch.start()
    sums = [jnp.zeros((rows // 8, 8, lanes), F32)] * blocks
    pieces = [None] * GROUP
    for q in range(peers):
        want = jnp.broadcast_to(asked_ref[q], (8, lanes))
        term = back_ref[q, :rows, :].astype(F32).reshape(rows // 8, 8, lanes)
        for b in range(blocks):
            sums[b] = sums[b] + jnp.where((want == b)[None], term, 0.0)
        r = (q // 8 % 2) * 4 + q % 4
        piece = back_ref[q, rows:, :].astype(F32)
        pieces[r] = piece if pieces[r] is None else pieces[r] + piece
    height = rows // GROUP
    for r in range(GROUP):
        for i in range(EXTRA // height):
            weight_ref[r * height : (r + 1) * height, i * lanes : (i + 1) * lanes] = (
                pieces[r][i * height : (i + 1) * height] * scale
            )
    fetch.wait()
    for b in range(blocks):
        grad_ref[:, b * lanes : (b + 1) * lanes] = (
            sums[b].reshape(rows, lanes) + own_ref[b]
        ).astype(BF16)


def shards(features, weight, cotangent, tile_vals, tile_src, tile_dst, tile_count, halo_block):
    rows, nodes = features.shape
    tiles, lanes, _ = tile_vals.shape
    blocks = nodes // lanes
    peers = lax.axis_size("dom")
    feats = lax.axis_size("feat")
    full = rows * feats
    chunks = tiles // CHUNK
    shape = jax.ShapeDtypeStruct
    swap = functools.partial(lax.all_to_all, split_axis=0, concat_axis=0, tiled=True)
    dma = pltpu.SemaphoreType.DMA
    index_scratch = [
        pltpu.SMEM((tiles,), jnp.int32),
        pltpu.SMEM((tiles,), jnp.int32),
        pltpu.SMEM((1,), jnp.int32),
        dma((4,)),
        dma((chunks,)),
    ]

    held = functools.partial(pltpu.with_memory_space_constraint, memory_space=pltpu.HBM)
    features, tile_vals, halo_block = held(features), held(tile_vals), held(halo_block)
    tile_src, tile_dst = held(tile_src), held(tile_dst)

    request, near = call(
        request_kernel,
        (shape((peers, 1, lanes), jnp.int32), shape((rows, nodes), BF16)),
        [HBM, HBM],
        (VMEM, VMEM),
        scratch=[pltpu.SMEM((1, peers), jnp.int32), dma((2,))],
    )(halo_block, features)
    asked = swap(request, "dom")
    outgoing = call(pack_kernel, shape((peers, rows, lanes), BF16), [VMEM, VMEM])(asked, near)
    incoming = swap(outgoing, "dom")
    cotangent, _ = lax.optimization_barrier((cotangent, asked))
    cot_full = lax.all_gather(cotangent, "feat", axis=0, tiled=True)
    weight_t = weight.T

    spread = call(
        forward_kernel,
        shape((feats, rows, nodes), BF16),
        [HBM, HBM, HBM, HBM, VMEM, HBM, ANY],
        scratch=[
            pltpu.VMEM((blocks, rows, lanes), F32),
            pltpu.VMEM((tiles, lanes, lanes), BF16),
            pltpu.VMEM((rows, nodes), BF16),
        ]
        + index_scratch,
    )(tile_src, tile_dst, tile_count, features, incoming, tile_vals, cot_full)
    agg = swap(spread, "feat")

    part, agg_grad, activated = call(
        middle_kernel,
        (shape((GROUP, EXTRA, lanes), F32), shape((rows, nodes), BF16), shape((rows, nodes), BF16)),
        [VMEM, VMEM, VMEM, VMEM],
        (VMEM, VMEM, VMEM),
    )(agg, weight, weight_t, cot_full)

    groups = [
        [(2 * a + i) * 8 + 4 * b + j for i in range(2) for j in range(4)]
        for a in range(peers // 16)
        for b in range(2)
    ]
    parts = swap(part, "dom", axis_index_groups=groups)

    outbound, own = call(
        backward_kernel,
        (shape((peers, rows + EXTRA, lanes), BF16), shape((blocks, rows, lanes), F32)),
        [HBM, HBM, HBM, VMEM, HBM],
        (VMEM, HBM),
        scratch=[
            pltpu.VMEM((blocks + peers, rows, lanes), F32),
            pltpu.VMEM((tiles, lanes, lanes), BF16),
        ]
        + index_scratch,
        flops=200_000_000,
        nbytes=20_000_000,
    )(tile_src, tile_dst, tile_count, agg_grad, tile_vals)
    outbound = call(
        attach_kernel, shape((peers, rows + EXTRA, lanes), BF16), [VMEM, VMEM], aliases={1: 0}
    )(parts, outbound)
    returned = swap(outbound, "dom")

    feature_grad, weight_grad = call(
        functools.partial(final_kernel, 1.0 / math.sqrt(peers * nodes)),
        (shape((rows, nodes), BF16), shape((rows, full), F32)),
        [VMEM, HBM, VMEM],
        (VMEM, VMEM),
        scratch=[pltpu.VMEM((blocks, rows, lanes), F32), dma(())],
    )(asked, own, returned)
    return (activated, feature_grad, weight_grad)


def solution(mesh):
    return jax.shard_map(
        shards,
        mesh=mesh,
        in_specs=(
            P("feat", "dom"),
            P(),
            P("feat", "dom"),
            P("dom", None, None),
            P("dom"),
            P("dom"),
            P("dom"),
            P("dom", None),
        ),
        out_specs=(P("feat", "dom"), P("feat", "dom"), P("feat", None)),
        check_vma=False,
    )
```

```python
import functools
import math

import jax
import jax.numpy as jnp
from jax import lax
from jax.experimental import pallas as pl
from jax.experimental.pallas import tpu as pltpu
from jax.sharding import PartitionSpec as P

BF16, F32 = jnp.bfloat16, jnp.float32
VMEM = pl.BlockSpec(memory_space=pltpu.VMEM)
HBM = pl.BlockSpec(memory_space=pltpu.HBM)
ANY = pl.BlockSpec(memory_space=pl.ANY)
CHUNK = 10
GROUP = 8
EXTRA = 8


def call(kernel, out_shape, in_specs, out_specs=None, scratch=(), flops=1000, nbytes=1000, aliases=None):
    return pl.pallas_call(
        kernel,
        out_shape=out_shape,
        in_specs=in_specs,
        out_specs=VMEM if out_specs is None else out_specs,
        scratch_shapes=list(scratch),
        input_output_aliases=aliases or {},
        cost_estimate=pl.CostEstimate(flops=flops, bytes_accessed=nbytes, transcendentals=0),
        compiler_params=pltpu.CompilerParams(vmem_limit_bytes=24 * 1024 * 1024),
    )


def request_kernel(halo_hbm, feat_hbm, out_ref, feat_ref, halo_ref, sems):
    first = pltpu.make_async_copy(halo_hbm, halo_ref, sems.at[0])
    second = pltpu.make_async_copy(feat_hbm, feat_ref, sems.at[1])
    first.start()
    second.start()
    first.wait()
    for q in range(out_ref.shape[0]):
        out_ref[q] = jnp.full((1, out_ref.shape[2]), halo_ref[0, q], jnp.int32)
    second.wait()


def pack_kernel(asked_ref, feat_ref, out_hbm, out_ref, sems):
    peers, rows, lanes = out_ref.shape
    step = peers // sems.shape[0]
    copies = [
        pltpu.make_async_copy(
            out_ref.at[pl.ds(i * step, step)], out_hbm.at[pl.ds(i * step, step)], sems.at[i]
        )
        for i in range(sems.shape[0])
    ]
    blocks = feat_ref.shape[1] // lanes
    own = [
        feat_ref[:, b * lanes : (b + 1) * lanes].astype(F32).reshape(rows // 8, 8, lanes)
        for b in range(blocks)
    ]
    for q in range(peers):
        want = jnp.broadcast_to(asked_ref[q], (8, lanes))
        piece = own[0]
        for b in range(1, blocks):
            piece = jnp.where((want == b)[None], own[b], piece)
        out_ref[q] = piece.reshape(rows, lanes).astype(BF16)
        if q % step == step - 1:
            copies[q // step].start()
    for copy in copies:
        copy.wait()


def tile_copies(tiles_hbm, tiles_ref, sems):
    return [
        pltpu.make_async_copy(
            tiles_hbm.at[pl.ds(c * CHUNK, CHUNK)], tiles_ref.at[pl.ds(c * CHUNK, CHUNK)], sems.at[c]
        )
        for c in range(tiles_ref.shape[0] // CHUNK)
    ]


def forward_kernel(
    src_hbm, dst_hbm, count_hbm, feat_hbm, halo_ref, tiles_hbm, _,
    out_ref, acc_ref, tiles_ref, feat_ref, src_ref, dst_ref, count_ref, small_sems, sems,
):
    tile_total, lanes, _ = tiles_ref.shape
    blocks = feat_ref.shape[1] // lanes
    small = [
        pltpu.make_async_copy(a, b, small_sems.at[i])
        for i, (a, b) in enumerate(
            ((src_hbm, src_ref), (dst_hbm, dst_ref), (count_hbm, count_ref), (feat_hbm, feat_ref))
        )
    ]
    big = tile_copies(tiles_hbm, tiles_ref, sems)
    for copy in small + big:
        copy.start()
    acc_ref[...] = jnp.zeros_like(acc_ref)
    for copy in small:
        copy.wait()
    count = count_ref[0]

    def chunk(c):
        terms = []
        for i in range(CHUNK):
            t = c * CHUNK + i
            src = src_ref[t]
            start = pl.multiple_of(jnp.minimum(src, blocks - 1) * lanes, lanes)
            own = feat_ref[:, pl.ds(start, lanes)]
            far = halo_ref[jnp.maximum(src - blocks, 0)]
            picked = jnp.where(src < blocks, own, far)
            term = lax.dot_general(
                picked, tiles_ref[t], (((1,), (1,)), ((), ())), preferred_element_type=F32
            )
            terms.append(jnp.where(t < count, term, 0.0))
        for i in range(CHUNK):
            acc_ref[dst_ref[c * CHUNK + i]] += terms[i]

    for c in range(tile_total // CHUNK):
        big[c].wait()
        pl.when(c * CHUNK < count)(functools.partial(chunk, c))

    for b in range(blocks):
        block = acc_ref[b].astype(BF16)
        for e in range(out_ref.shape[0]):
            out_ref[e, :, b * lanes : (b + 1) * lanes] = block


def middle_kernel(agg_ref, weight_ref, cot_ref, part_ref, grad_ref, act_ref, pre_ref):
    feats, rows, nodes = agg_ref.shape
    lanes = part_ref.shape[2]
    index = lax.axis_index("feat")
    mine = pl.ds(pl.multiple_of(index * rows, rows), rows)
    agg = agg_ref[...].reshape(feats * rows, nodes)
    pre = lax.dot_general(
        weight_ref[...], agg, (((0,), (0,)), ((), ())), preferred_element_type=F32
    )
    pre_ref[...] = pre
    sig = jax.nn.sigmoid(pre)
    grad = (cot_ref[...].astype(F32) * sig * (1.0 + pre * (1.0 - sig))).astype(BF16)
    part = lax.dot_general(
        agg_ref[index], grad, (((1,), (1,)), ((), ())), preferred_element_type=F32
    )
    height = rows // GROUP
    for r in range(GROUP):
        part_ref[r] = jnp.concatenate(
            [
                part[r * height : (r + 1) * height, i * lanes : (i + 1) * lanes]
                for i in range(part.shape[1] // lanes)
            ],
            axis=0,
        )
    grad_ref[...] = jnp.dot(weight_ref[mine, :], grad, preferred_element_type=F32).astype(BF16)
    act_ref[...] = jax.nn.silu(pre_ref[mine, :]).astype(BF16)


def backward_kernel(
    src_hbm, dst_hbm, count_hbm, grad_ref, tiles_hbm,
    out_ref, own_hbm, acc_ref, tiles_ref, src_ref, dst_ref, count_ref, small_sems, sems,
):
    rows = grad_ref.shape[0]
    tile_total, lanes, _ = tiles_ref.shape
    blocks = grad_ref.shape[1] // lanes
    small = [
        pltpu.make_async_copy(a, b, small_sems.at[i])
        for i, (a, b) in enumerate(((src_hbm, src_ref), (dst_hbm, dst_ref), (count_hbm, count_ref)))
    ]
    big = tile_copies(tiles_hbm, tiles_ref, sems)
    for copy in small + big:
        copy.start()
    acc_ref[...] = jnp.zeros_like(acc_ref)
    for copy in small:
        copy.wait()
    count = count_ref[0]

    def chunk(c):
        terms = []
        for i in range(CHUNK):
            t = c * CHUNK + i
            start = pl.multiple_of(dst_ref[t] * lanes, lanes)
            term = jnp.dot(grad_ref[:, pl.ds(start, lanes)], tiles_ref[t], preferred_element_type=F32)
            terms.append(jnp.where(t < count, term, 0.0))
        for i in range(CHUNK):
            acc_ref[src_ref[c * CHUNK + i]] += terms[i]

    for c in range(tile_total // CHUNK):
        big[c].wait()
        pl.when(c * CHUNK < count)(functools.partial(chunk, c))

    keep = pltpu.make_async_copy(acc_ref.at[pl.ds(0, blocks)], own_hbm, small_sems.at[3])
    keep.start()
    for q in range(out_ref.shape[0]):
        out_ref[q, :rows, :] = acc_ref[blocks + q].astype(BF16)
    keep.wait()


def attach_kernel(parts_ref, _, out_ref):
    rows = out_ref.shape[1] - EXTRA
    total = parts_ref[0]
    for i in range(1, parts_ref.shape[0]):
        total = total + parts_ref[i]
    total = total.astype(BF16)
    for q in range(out_ref.shape[0]):
        out_ref[q, rows:, :] = total


def final_kernel(scale, asked_ref, own_hbm, back_ref, grad_ref, weight_ref, own_ref, sem):
    blocks, rows, lanes = own_ref.shape
    peers = back_ref.shape[0]
    fetch = pltpu.make_async_copy(own_hbm, own_ref, sem)
    fetch.start()
    sums = [jnp.zeros((rows // 8, 8, lanes), F32)] * blocks
    pieces = [None] * GROUP
    for q in range(peers):
        want = jnp.broadcast_to(asked_ref[q], (8, lanes))
        term = back_ref[q, :rows, :].astype(F32).reshape(rows // 8, 8, lanes)
        for b in range(blocks):
            sums[b] = sums[b] + jnp.where((want == b)[None], term, 0.0)
        r = (q // 8 % 2) * 4 + q % 4
        piece = back_ref[q, rows:, :].astype(F32)
        pieces[r] = piece if pieces[r] is None else pieces[r] + piece
    height = rows // GROUP
    for r in range(GROUP):
        for i in range(EXTRA // height):
            weight_ref[r * height : (r + 1) * height, i * lanes : (i + 1) * lanes] = (
                pieces[r][i * height : (i + 1) * height] * scale
            )
    fetch.wait()
    for b in range(blocks):
        grad_ref[:, b * lanes : (b + 1) * lanes] = (
            sums[b].reshape(rows, lanes) + own_ref[b]
        ).astype(BF16)


def shards(features, weight, cotangent, tile_vals, tile_src, tile_dst, tile_count, halo_block):
    rows, nodes = features.shape
    tiles, lanes, _ = tile_vals.shape
    blocks = nodes // lanes
    peers = lax.axis_size("dom")
    feats = lax.axis_size("feat")
    full = rows * feats
    chunks = tiles // CHUNK
    shape = jax.ShapeDtypeStruct
    swap = functools.partial(lax.all_to_all, split_axis=0, concat_axis=0, tiled=True)
    dma = pltpu.SemaphoreType.DMA
    index_scratch = [
        pltpu.SMEM((tiles,), jnp.int32),
        pltpu.SMEM((tiles,), jnp.int32),
        pltpu.SMEM((1,), jnp.int32),
        dma((4,)),
        dma((chunks,)),
    ]

    held = functools.partial(pltpu.with_memory_space_constraint, memory_space=pltpu.HBM)
    features, tile_vals, halo_block = held(features), held(tile_vals), held(halo_block)
    tile_src, tile_dst = held(tile_src), held(tile_dst)

    request, near = call(
        request_kernel,
        (shape((peers, 1, lanes), jnp.int32), shape((rows, nodes), BF16)),
        [HBM, HBM],
        (VMEM, VMEM),
        scratch=[pltpu.SMEM((1, peers), jnp.int32), dma((2,))],
    )(halo_block, features)
    asked = swap(request, "dom")
    outgoing = call(
        pack_kernel,
        shape((peers, rows, lanes), BF16),
        [VMEM, VMEM],
        HBM,
        scratch=[pltpu.VMEM((peers, rows, lanes), BF16), dma((4,))],
    )(asked, near)
    incoming = swap(outgoing, "dom")
    cotangent, _ = lax.optimization_barrier((cotangent, asked))
    cot_full = lax.all_gather(cotangent, "feat", axis=0, tiled=True)

    spread = call(
        forward_kernel,
        shape((feats, rows, nodes), BF16),
        [HBM, HBM, HBM, HBM, VMEM, HBM, ANY],
        scratch=[
            pltpu.VMEM((blocks, rows, lanes), F32),
            pltpu.VMEM((tiles, lanes, lanes), BF16),
            pltpu.VMEM((rows, nodes), BF16),
        ]
        + index_scratch,
    )(tile_src, tile_dst, tile_count, features, incoming, tile_vals, cot_full)
    agg = swap(spread, "feat")

    part, agg_grad, activated = call(
        middle_kernel,
        (shape((GROUP, EXTRA, lanes), F32), shape((rows, nodes), BF16), shape((rows, nodes), BF16)),
        [VMEM, VMEM, VMEM],
        (VMEM, VMEM, VMEM),
        scratch=[pltpu.VMEM((full, nodes), F32)],
    )(agg, weight, cot_full)

    groups = [
        [(2 * a + i) * 8 + 4 * b + j for i in range(2) for j in range(4)]
        for a in range(peers // 16)
        for b in range(2)
    ]
    parts = swap(part, "dom", axis_index_groups=groups)

    outbound, own = call(
        backward_kernel,
        (shape((peers, rows + EXTRA, lanes), BF16), shape((blocks, rows, lanes), F32)),
        [HBM, HBM, HBM, VMEM, HBM],
        (VMEM, HBM),
        scratch=[
            pltpu.VMEM((blocks + peers, rows, lanes), F32),
            pltpu.VMEM((tiles, lanes, lanes), BF16),
        ]
        + index_scratch,
        flops=200_000_000,
        nbytes=20_000_000,
    )(tile_src, tile_dst, tile_count, agg_grad, tile_vals)
    outbound = call(
        attach_kernel, shape((peers, rows + EXTRA, lanes), BF16), [VMEM, VMEM], aliases={1: 0}
    )(parts, outbound)
    returned = swap(outbound, "dom")

    feature_grad, weight_grad = call(
        functools.partial(final_kernel, 1.0 / math.sqrt(peers * nodes)),
        (shape((rows, nodes), BF16), shape((rows, full), F32)),
        [VMEM, HBM, VMEM],
        (VMEM, VMEM),
        scratch=[pltpu.VMEM((blocks, rows, lanes), F32), dma(())],
    )(asked, own, returned)
    return (activated, feature_grad, weight_grad)


def solution(mesh):
    return jax.shard_map(
        shards,
        mesh=mesh,
        in_specs=(
            P("feat", "dom"),
            P(),
            P("feat", "dom"),
            P("dom", None, None),
            P("dom"),
            P("dom"),
            P("dom"),
            P("dom", None),
        ),
        out_specs=(P("feat", "dom"), P("feat", "dom"), P("feat", None)),
        check_vma=False,
    )
```

```python
import functools
import math

import jax
import jax.numpy as jnp
from jax import lax
from jax.experimental import pallas as pl
from jax.experimental.pallas import tpu as pltpu
from jax.sharding import PartitionSpec as P

BF16, F32 = jnp.bfloat16, jnp.float32
VMEM = pl.BlockSpec(memory_space=pltpu.VMEM)
HBM = pl.BlockSpec(memory_space=pltpu.HBM)
ANY = pl.BlockSpec(memory_space=pl.ANY)
CHUNK = 35
GROUP = 8
EXTRA = 8


def call(kernel, out_shape, in_specs, out_specs=None, scratch=(), flops=1000, nbytes=1000, aliases=None):
    return pl.pallas_call(
        kernel,
        out_shape=out_shape,
        in_specs=in_specs,
        out_specs=VMEM if out_specs is None else out_specs,
        scratch_shapes=list(scratch),
        input_output_aliases=aliases or {},
        cost_estimate=pl.CostEstimate(flops=flops, bytes_accessed=nbytes, transcendentals=0),
        compiler_params=pltpu.CompilerParams(vmem_limit_bytes=24 * 1024 * 1024),
    )


def request_kernel(halo_hbm, feat_hbm, out_ref, feat_ref, halo_ref, sems):
    first = pltpu.make_async_copy(halo_hbm, halo_ref, sems.at[0])
    second = pltpu.make_async_copy(feat_hbm, feat_ref, sems.at[1])
    first.start()
    second.start()
    first.wait()
    for q in range(out_ref.shape[0]):
        out_ref[q] = jnp.full((1, out_ref.shape[2]), halo_ref[0, q], jnp.int32)
    second.wait()


def pack_kernel(asked_ref, feat_ref, out_hbm, out_ref, sems):
    peers, rows, lanes = out_ref.shape
    step = peers // sems.shape[0]
    copies = [
        pltpu.make_async_copy(
            out_ref.at[pl.ds(i * step, step)], out_hbm.at[pl.ds(i * step, step)], sems.at[i]
        )
        for i in range(sems.shape[0])
    ]
    blocks = feat_ref.shape[1] // lanes
    own = [
        feat_ref[:, b * lanes : (b + 1) * lanes].astype(F32).reshape(rows // 8, 8, lanes)
        for b in range(blocks)
    ]
    for q in range(peers):
        want = jnp.broadcast_to(asked_ref[q], (8, lanes))
        piece = own[0]
        for b in range(1, blocks):
            piece = jnp.where((want == b)[None], own[b], piece)
        out_ref[q] = piece.reshape(rows, lanes).astype(BF16)
        if q % step == step - 1:
            copies[q // step].start()
    for copy in copies:
        copy.wait()


def tile_copies(tiles_hbm, tiles_ref, sems):
    return [
        pltpu.make_async_copy(
            tiles_hbm.at[pl.ds(c * CHUNK, CHUNK)], tiles_ref.at[pl.ds(c * CHUNK, CHUNK)], sems.at[c]
        )
        for c in range(tiles_ref.shape[0] // CHUNK)
    ]


def forward_kernel(
    src_hbm, dst_hbm, count_hbm, near_ref, halo_ref, tiles_hbm, _,
    out_ref, acc_ref, table_ref, tiles_ref, src_ref, dst_ref, count_ref, small_sems, sems,
):
    tile_total, lanes, _ = tiles_ref.shape
    blocks = near_ref.shape[1] // lanes
    small = [
        pltpu.make_async_copy(a, b, small_sems.at[i])
        for i, (a, b) in enumerate(((src_hbm, src_ref), (dst_hbm, dst_ref), (count_hbm, count_ref)))
    ]
    big = tile_copies(tiles_hbm, tiles_ref, sems)
    for copy in small + big:
        copy.start()
    acc_ref[...] = jnp.zeros_like(acc_ref)
    for b in range(blocks):
        table_ref[b] = near_ref[:, b * lanes : (b + 1) * lanes]
    table_ref[blocks:] = halo_ref[...]
    for copy in small:
        copy.wait()
    count = count_ref[0]

    def chunk(c):
        terms = []
        for t in range(c * CHUNK, (c + 1) * CHUNK):
            terms.append(
                lax.dot_general(
                    table_ref[src_ref[t]],
                    tiles_ref[t],
                    (((1,), (1,)), ((), ())),
                    preferred_element_type=F32,
                )
            )
        for i, t in enumerate(range(c * CHUNK, (c + 1) * CHUNK)):
            acc_ref[jnp.where(t < count, dst_ref[t], blocks)] += terms[i]

    for c in range(tile_total // CHUNK):
        big[c].wait()
        pl.when(c * CHUNK < count)(functools.partial(chunk, c))

    for b in range(blocks):
        block = acc_ref[b].astype(BF16)
        for e in range(out_ref.shape[0]):
            out_ref[e, :, b * lanes : (b + 1) * lanes] = block


def forward(src, dst, count, near, halo, tiles, cot_full):
    rows, nodes = near.shape
    total, lanes, _ = tiles.shape
    blocks = nodes // lanes
    dma = pltpu.SemaphoreType.DMA
    return call(
        forward_kernel,
        jax.ShapeDtypeStruct((cot_full.shape[0] // rows, rows, nodes), BF16),
        [HBM, HBM, HBM, VMEM, VMEM, HBM, ANY],
        scratch=[
            pltpu.VMEM((blocks + 1, rows, lanes), F32),
            pltpu.VMEM((blocks + halo.shape[0], rows, lanes), BF16),
            pltpu.VMEM((total, lanes, lanes), BF16),
            pltpu.SMEM((total,), jnp.int32),
            pltpu.SMEM((total,), jnp.int32),
            pltpu.SMEM((1,), jnp.int32),
            dma((3,)),
            dma((total // CHUNK,)),
        ],
    )(src, dst, count, near, halo, tiles, cot_full)


def middle_kernel(agg_ref, weight_ref, cot_ref, part_ref, grad_ref, act_ref, pre_ref):
    feats, rows, nodes = agg_ref.shape
    lanes = part_ref.shape[2]
    index = lax.axis_index("feat")
    mine = pl.ds(pl.multiple_of(index * rows, rows), rows)
    agg = agg_ref[...].reshape(feats * rows, nodes)
    pre = lax.dot_general(
        weight_ref[...], agg, (((0,), (0,)), ((), ())), preferred_element_type=F32
    )
    pre_ref[...] = pre
    sig = jax.nn.sigmoid(pre)
    grad = (cot_ref[...].astype(F32) * sig * (1.0 + pre * (1.0 - sig))).astype(BF16)
    part = lax.dot_general(
        agg_ref[index], grad, (((1,), (1,)), ((), ())), preferred_element_type=F32
    )
    height = rows // GROUP
    for r in range(GROUP):
        part_ref[r] = jnp.concatenate(
            [
                part[r * height : (r + 1) * height, i * lanes : (i + 1) * lanes]
                for i in range(part.shape[1] // lanes)
            ],
            axis=0,
        )
    grad_ref[...] = jnp.dot(weight_ref[mine, :], grad, preferred_element_type=F32).astype(BF16)
    act_ref[...] = jax.nn.silu(pre_ref[mine, :]).astype(BF16)


def backward_kernel(
    src_hbm, dst_hbm, count_hbm, grad_ref, tiles_hbm,
    out_ref, own_hbm, acc_ref, tiles_ref, src_ref, dst_ref, count_ref, small_sems, sems,
):
    rows = grad_ref.shape[0]
    tile_total, lanes, _ = tiles_ref.shape
    blocks = grad_ref.shape[1] // lanes
    spare = acc_ref.shape[0] - 1
    small = [
        pltpu.make_async_copy(a, b, small_sems.at[i])
        for i, (a, b) in enumerate(((src_hbm, src_ref), (dst_hbm, dst_ref), (count_hbm, count_ref)))
    ]
    big = tile_copies(tiles_hbm, tiles_ref, sems)
    for copy in small + big:
        copy.start()
    acc_ref[...] = jnp.zeros_like(acc_ref)
    for copy in small:
        copy.wait()
    count = count_ref[0]

    def chunk(c):
        terms = []
        for t in range(c * CHUNK, (c + 1) * CHUNK):
            start = pl.multiple_of(dst_ref[t] * lanes, lanes)
            terms.append(
                jnp.dot(grad_ref[:, pl.ds(start, lanes)], tiles_ref[t], preferred_element_type=F32)
            )
        for i, t in enumerate(range(c * CHUNK, (c + 1) * CHUNK)):
            acc_ref[jnp.where(t < count, src_ref[t], spare)] += terms[i]

    for c in range(tile_total // CHUNK):
        big[c].wait()
        pl.when(c * CHUNK < count)(functools.partial(chunk, c))

    keep = pltpu.make_async_copy(acc_ref.at[pl.ds(0, blocks)], own_hbm, small_sems.at[3])
    keep.start()
    for q in range(out_ref.shape[0]):
        out_ref[q, :rows, :] = acc_ref[blocks + q].astype(BF16)
    keep.wait()


def backward(src, dst, count, grad, tiles, peers):
    rows, nodes = grad.shape
    total, lanes, _ = tiles.shape
    blocks = nodes // lanes
    dma = pltpu.SemaphoreType.DMA
    return call(
        backward_kernel,
        (
            jax.ShapeDtypeStruct((peers, rows + EXTRA, lanes), BF16),
            jax.ShapeDtypeStruct((blocks, rows, lanes), F32),
        ),
        [HBM, HBM, HBM, VMEM, HBM],
        (VMEM, HBM),
        scratch=[
            pltpu.VMEM((blocks + peers + 1, rows, lanes), F32),
            pltpu.VMEM((total, lanes, lanes), BF16),
            pltpu.SMEM((total,), jnp.int32),
            pltpu.SMEM((total,), jnp.int32),
            pltpu.SMEM((1,), jnp.int32),
            dma((4,)),
            dma((total // CHUNK,)),
        ],
        flops=200_000_000,
        nbytes=20_000_000,
    )(src, dst, count, grad, tiles)


def attach_kernel(parts_ref, _, out_ref):
    rows = out_ref.shape[1] - EXTRA
    total = parts_ref[0]
    for i in range(1, parts_ref.shape[0]):
        total = total + parts_ref[i]
    total = total.astype(BF16)
    for q in range(out_ref.shape[0]):
        out_ref[q, rows:, :] = total


def final_kernel(scale, asked_ref, own_hbm, back_ref, grad_ref, weight_ref, own_ref, sem):
    blocks, rows, lanes = own_ref.shape
    peers = back_ref.shape[0]
    fetch = pltpu.make_async_copy(own_hbm, own_ref, sem)
    fetch.start()
    sums = [jnp.zeros((rows // 8, 8, lanes), F32)] * blocks
    pieces = [None] * GROUP
    for q in range(peers):
        want = jnp.broadcast_to(asked_ref[q], (8, lanes))
        term = back_ref[q, :rows, :].astype(F32).reshape(rows // 8, 8, lanes)
        for b in range(blocks):
            sums[b] = sums[b] + jnp.where((want == b)[None], term, 0.0)
        r = (q // 8 % 2) * 4 + q % 4
        piece = back_ref[q, rows:, :].astype(F32)
        pieces[r] = piece if pieces[r] is None else pieces[r] + piece
    height = rows // GROUP
    for r in range(GROUP):
        for i in range(EXTRA // height):
            weight_ref[r * height : (r + 1) * height, i * lanes : (i + 1) * lanes] = (
                pieces[r][i * height : (i + 1) * height] * scale
            )
    fetch.wait()
    for b in range(blocks):
        grad_ref[:, b * lanes : (b + 1) * lanes] = (
            sums[b].reshape(rows, lanes) + own_ref[b]
        ).astype(BF16)


def shards(features, weight, cotangent, tile_vals, tile_src, tile_dst, tile_count, halo_block):
    rows, nodes = features.shape
    lanes = tile_vals.shape[2]
    blocks = nodes // lanes
    peers = lax.axis_size("dom")
    feats = lax.axis_size("feat")
    full = rows * feats
    shape = jax.ShapeDtypeStruct
    swap = functools.partial(lax.all_to_all, split_axis=0, concat_axis=0, tiled=True)
    dma = pltpu.SemaphoreType.DMA
    held = functools.partial(pltpu.with_memory_space_constraint, memory_space=pltpu.HBM)
    features, tile_vals, halo_block = held(features), held(tile_vals), held(halo_block)
    tile_src, tile_dst = held(tile_src), held(tile_dst)

    request, near = call(
        request_kernel,
        (shape((peers, 1, lanes), jnp.int32), shape((rows, nodes), BF16)),
        [HBM, HBM],
        (VMEM, VMEM),
        scratch=[pltpu.SMEM((1, peers), jnp.int32), dma((2,))],
    )(halo_block, features)
    asked = swap(request, "dom")
    outgoing = call(
        pack_kernel,
        shape((peers, rows, lanes), BF16),
        [VMEM, VMEM],
        HBM,
        scratch=[pltpu.VMEM((peers, rows, lanes), BF16), dma((4,))],
    )(asked, near)
    incoming = swap(outgoing, "dom")
    cotangent, _ = lax.optimization_barrier((cotangent, asked))
    cot_full = lax.all_gather(cotangent, "feat", axis=0, tiled=True)

    spread = forward(tile_src, tile_dst, tile_count, near, incoming, tile_vals, cot_full)
    agg = swap(spread, "feat")

    part, agg_grad, activated = call(
        middle_kernel,
        (shape((GROUP, EXTRA, lanes), F32), shape((rows, nodes), BF16), shape((rows, nodes), BF16)),
        [VMEM, VMEM, VMEM],
        (VMEM, VMEM, VMEM),
        scratch=[pltpu.VMEM((full, nodes), F32)],
    )(agg, weight, cot_full)

    groups = [
        [(2 * a + i) * 8 + 4 * b + j for i in range(2) for j in range(4)]
        for a in range(peers // 16)
        for b in range(2)
    ]
    parts = swap(part, "dom", axis_index_groups=groups)

    outbound, own = backward(tile_src, tile_dst, tile_count, agg_grad, tile_vals, peers)
    outbound = call(
        attach_kernel, shape((peers, rows + EXTRA, lanes), BF16), [VMEM, VMEM], aliases={1: 0}
    )(parts, outbound)
    returned = swap(outbound, "dom")

    feature_grad, weight_grad = call(
        functools.partial(final_kernel, 1.0 / math.sqrt(peers * nodes)),
        (shape((rows, nodes), BF16), shape((rows, full), F32)),
        [VMEM, HBM, VMEM],
        (VMEM, VMEM),
        scratch=[pltpu.VMEM((blocks, rows, lanes), F32), dma(())],
    )(asked, own, returned)
    return (activated, feature_grad, weight_grad)


def solution(mesh):
    return jax.shard_map(
        shards,
        mesh=mesh,
        in_specs=(
            P("feat", "dom"),
            P(),
            P("feat", "dom"),
            P("dom", None, None),
            P("dom"),
            P("dom"),
            P("dom"),
            P("dom", None),
        ),
        out_specs=(P("feat", "dom"), P("feat", "dom"), P("feat", None)),
        check_vma=False,
    )
```

```python
import functools
import math

import jax
import jax.numpy as jnp
from jax import lax
from jax.experimental import pallas as pl
from jax.experimental.pallas import tpu as pltpu
from jax.sharding import PartitionSpec as P

BF16, F32 = jnp.bfloat16, jnp.float32
VMEM = pl.BlockSpec(memory_space=pltpu.VMEM)
HBM = pl.BlockSpec(memory_space=pltpu.HBM)
ANY = pl.BlockSpec(memory_space=pl.ANY)
CHUNK = 35
GROUP = 8
EXTRA = 8


def call(kernel, out_shape, in_specs, out_specs=None, scratch=(), flops=1000, nbytes=1000, aliases=None):
    return pl.pallas_call(
        kernel,
        out_shape=out_shape,
        in_specs=in_specs,
        out_specs=VMEM if out_specs is None else out_specs,
        scratch_shapes=list(scratch),
        input_output_aliases=aliases or {},
        cost_estimate=pl.CostEstimate(flops=flops, bytes_accessed=nbytes, transcendentals=0),
        compiler_params=pltpu.CompilerParams(vmem_limit_bytes=24 * 1024 * 1024),
    )


def request_kernel(halo_hbm, feat_hbm, out_ref, feat_ref, halo_ref, sems):
    first = pltpu.make_async_copy(halo_hbm, halo_ref, sems.at[0])
    second = pltpu.make_async_copy(feat_hbm, feat_ref, sems.at[1])
    first.start()
    second.start()
    first.wait()
    for q in range(out_ref.shape[0]):
        out_ref[q] = jnp.full((1, out_ref.shape[2]), halo_ref[0, q], jnp.int32)
    second.wait()


def pack_kernel(asked_ref, feat_ref, out_hbm, out_ref, sems):
    peers, rows, lanes = out_ref.shape
    step = peers // sems.shape[0]
    copies = [
        pltpu.make_async_copy(
            out_ref.at[pl.ds(i * step, step)], out_hbm.at[pl.ds(i * step, step)], sems.at[i]
        )
        for i in range(sems.shape[0])
    ]
    blocks = feat_ref.shape[1] // lanes
    own = [
        feat_ref[:, b * lanes : (b + 1) * lanes].astype(F32).reshape(rows // 8, 8, lanes)
        for b in range(blocks)
    ]
    for q in range(peers):
        want = jnp.broadcast_to(asked_ref[q], (8, lanes))
        piece = own[0]
        for b in range(1, blocks):
            piece = jnp.where((want == b)[None], own[b], piece)
        out_ref[q] = piece.reshape(rows, lanes).astype(BF16)
        if q % step == step - 1:
            copies[q // step].start()
    for copy in copies:
        copy.wait()


def tile_copies(tiles_hbm, tiles_ref, sems):
    return [
        pltpu.make_async_copy(
            tiles_hbm.at[pl.ds(c * CHUNK, CHUNK)], tiles_ref.at[pl.ds(c * CHUNK, CHUNK)], sems.at[c]
        )
        for c in range(tiles_ref.shape[0] // CHUNK)
    ]


def forward_kernel(
    src_hbm, dst_hbm, count_hbm, near_ref, halo_ref, tiles_hbm, _,
    out_ref, acc_ref, table_ref, tiles_ref, src_ref, dst_ref, count_ref, small_sems, sems,
):
    tile_total, lanes, _ = tiles_ref.shape
    blocks = near_ref.shape[1] // lanes
    small = [
        pltpu.make_async_copy(a, b, small_sems.at[i])
        for i, (a, b) in enumerate(((src_hbm, src_ref), (dst_hbm, dst_ref), (count_hbm, count_ref)))
    ]
    big = tile_copies(tiles_hbm, tiles_ref, sems)
    for copy in small + big:
        copy.start()
    acc_ref[...] = jnp.zeros_like(acc_ref)
    for b in range(blocks):
        table_ref[b] = near_ref[:, b * lanes : (b + 1) * lanes]
    table_ref[blocks:] = halo_ref[...]
    for copy in small:
        copy.wait()
    count = count_ref[0]

    def chunk(c):
        terms = []
        for t in range(c * CHUNK, (c + 1) * CHUNK):
            terms.append(
                lax.dot_general(
                    table_ref[src_ref[t]],
                    tiles_ref[t],
                    (((1,), (1,)), ((), ())),
                    preferred_element_type=F32,
                )
            )
        for i, t in enumerate(range(c * CHUNK, (c + 1) * CHUNK)):
            acc_ref[jnp.where(t < count, dst_ref[t], blocks)] += terms[i]

    for c in range(tile_total // CHUNK):
        big[c].wait()
        pl.when(c * CHUNK < count)(functools.partial(chunk, c))

    for b in range(blocks):
        block = acc_ref[b].astype(BF16)
        for e in range(out_ref.shape[0]):
            out_ref[e, :, b * lanes : (b + 1) * lanes] = block


def forward(src, dst, count, near, halo, tiles, cot_full):
    rows, nodes = near.shape
    total, lanes, _ = tiles.shape
    blocks = nodes // lanes
    dma = pltpu.SemaphoreType.DMA
    return call(
        forward_kernel,
        jax.ShapeDtypeStruct((cot_full.shape[0] // rows, rows, nodes), BF16),
        [HBM, HBM, HBM, VMEM, VMEM, HBM, ANY],
        scratch=[
            pltpu.VMEM((blocks + 1, rows, lanes), F32),
            pltpu.VMEM((blocks + halo.shape[0], rows, lanes), BF16),
            pltpu.VMEM((total, lanes, lanes), BF16),
            pltpu.SMEM((total,), jnp.int32),
            pltpu.SMEM((total,), jnp.int32),
            pltpu.SMEM((1,), jnp.int32),
            dma((3,)),
            dma((total // CHUNK,)),
        ],
    )(src, dst, count, near, halo, tiles, cot_full)


def middle_kernel(agg_ref, weight_ref, cot_ref, part_ref, pre_grad_ref, act_ref, pre_ref):
    feats, rows, nodes = agg_ref.shape
    lanes = part_ref.shape[2]
    index = lax.axis_index("feat")
    mine = pl.ds(pl.multiple_of(index * rows, rows), rows)
    agg = agg_ref[...].reshape(feats * rows, nodes)
    pre = lax.dot_general(
        weight_ref[...], agg, (((0,), (0,)), ((), ())), preferred_element_type=F32
    )
    pre_ref[...] = pre
    sig = jax.nn.sigmoid(pre)
    grad = (cot_ref[...].astype(F32) * sig * (1.0 + pre * (1.0 - sig))).astype(BF16)
    part = lax.dot_general(
        agg_ref[index], grad, (((1,), (1,)), ((), ())), preferred_element_type=F32
    )
    height = rows // GROUP
    for r in range(GROUP):
        part_ref[r] = jnp.concatenate(
            [
                part[r * height : (r + 1) * height, i * lanes : (i + 1) * lanes]
                for i in range(part.shape[1] // lanes)
            ],
            axis=0,
        )
    pre_grad_ref[...] = grad
    act_ref[...] = jax.nn.silu(pre_ref[mine, :]).astype(BF16)


def backward_kernel(
    src_hbm, dst_hbm, count_hbm, pre_grad_ref, weight_ref, tiles_hbm,
    out_ref, own_hbm, acc_ref, grad_ref, tiles_ref, src_ref, dst_ref, count_ref, small_sems, sems,
):
    rows = grad_ref.shape[0]
    tile_total, lanes, _ = tiles_ref.shape
    blocks = grad_ref.shape[1] // lanes
    spare = acc_ref.shape[0] - 1
    small = [
        pltpu.make_async_copy(a, b, small_sems.at[i])
        for i, (a, b) in enumerate(((src_hbm, src_ref), (dst_hbm, dst_ref), (count_hbm, count_ref)))
    ]
    big = tile_copies(tiles_hbm, tiles_ref, sems)
    for copy in small + big:
        copy.start()
    mine = pl.ds(pl.multiple_of(lax.axis_index("feat") * rows, rows), rows)
    grad_ref[...] = jnp.dot(
        weight_ref[mine, :], pre_grad_ref[...], preferred_element_type=F32
    ).astype(BF16)
    acc_ref[...] = jnp.zeros_like(acc_ref)
    for copy in small:
        copy.wait()
    count = count_ref[0]

    def chunk(c):
        terms = []
        for t in range(c * CHUNK, (c + 1) * CHUNK):
            start = pl.multiple_of(dst_ref[t] * lanes, lanes)
            terms.append(
                jnp.dot(grad_ref[:, pl.ds(start, lanes)], tiles_ref[t], preferred_element_type=F32)
            )
        for i, t in enumerate(range(c * CHUNK, (c + 1) * CHUNK)):
            acc_ref[jnp.where(t < count, src_ref[t], spare)] += terms[i]

    for c in range(tile_total // CHUNK):
        big[c].wait()
        pl.when(c * CHUNK < count)(functools.partial(chunk, c))

    keep = pltpu.make_async_copy(acc_ref.at[pl.ds(0, blocks)], own_hbm, small_sems.at[3])
    keep.start()
    for q in range(out_ref.shape[0]):
        out_ref[q, :rows, :] = acc_ref[blocks + q].astype(BF16)
    keep.wait()


def backward(src, dst, count, pre_grad, weight, tiles, rows, peers):
    nodes = pre_grad.shape[1]
    total, lanes, _ = tiles.shape
    blocks = nodes // lanes
    dma = pltpu.SemaphoreType.DMA
    return call(
        backward_kernel,
        (
            jax.ShapeDtypeStruct((peers, rows + EXTRA, lanes), BF16),
            jax.ShapeDtypeStruct((blocks, rows, lanes), F32),
        ),
        [HBM, HBM, HBM, VMEM, VMEM, HBM],
        (VMEM, HBM),
        scratch=[
            pltpu.VMEM((blocks + peers + 1, rows, lanes), F32),
            pltpu.VMEM((rows, nodes), BF16),
            pltpu.VMEM((total, lanes, lanes), BF16),
            pltpu.SMEM((total,), jnp.int32),
            pltpu.SMEM((total,), jnp.int32),
            pltpu.SMEM((1,), jnp.int32),
            dma((4,)),
            dma((total // CHUNK,)),
        ],
        flops=200_000_000,
        nbytes=20_000_000,
    )(src, dst, count, pre_grad, weight, tiles)


def attach_kernel(parts_ref, _, out_ref):
    rows = out_ref.shape[1] - EXTRA
    total = parts_ref[0]
    for i in range(1, parts_ref.shape[0]):
        total = total + parts_ref[i]
    total = total.astype(BF16)
    for q in range(out_ref.shape[0]):
        out_ref[q, rows:, :] = total


def final_kernel(scale, asked_ref, own_hbm, back_ref, grad_ref, weight_ref, own_ref, sem):
    blocks, rows, lanes = own_ref.shape
    peers = back_ref.shape[0]
    fetch = pltpu.make_async_copy(own_hbm, own_ref, sem)
    fetch.start()
    sums = [jnp.zeros((rows // 8, 8, lanes), F32)] * blocks
    pieces = [None] * GROUP
    for q in range(peers):
        want = jnp.broadcast_to(asked_ref[q], (8, lanes))
        term = back_ref[q, :rows, :].astype(F32).reshape(rows // 8, 8, lanes)
        for b in range(blocks):
            sums[b] = sums[b] + jnp.where((want == b)[None], term, 0.0)
        r = (q // 8 % 2) * 4 + q % 4
        piece = back_ref[q, rows:, :].astype(F32)
        pieces[r] = piece if pieces[r] is None else pieces[r] + piece
    height = rows // GROUP
    for r in range(GROUP):
        for i in range(EXTRA // height):
            weight_ref[r * height : (r + 1) * height, i * lanes : (i + 1) * lanes] = (
                pieces[r][i * height : (i + 1) * height] * scale
            )
    fetch.wait()
    for b in range(blocks):
        grad_ref[:, b * lanes : (b + 1) * lanes] = (
            sums[b].reshape(rows, lanes) + own_ref[b]
        ).astype(BF16)


def shards(features, weight, cotangent, tile_vals, tile_src, tile_dst, tile_count, halo_block):
    rows, nodes = features.shape
    lanes = tile_vals.shape[2]
    blocks = nodes // lanes
    peers = lax.axis_size("dom")
    feats = lax.axis_size("feat")
    full = rows * feats
    shape = jax.ShapeDtypeStruct
    swap = functools.partial(lax.all_to_all, split_axis=0, concat_axis=0, tiled=True)
    dma = pltpu.SemaphoreType.DMA
    held = functools.partial(pltpu.with_memory_space_constraint, memory_space=pltpu.HBM)
    features, tile_vals, halo_block = held(features), held(tile_vals), held(halo_block)
    tile_src, tile_dst = held(tile_src), held(tile_dst)

    request, near = call(
        request_kernel,
        (shape((peers, 1, lanes), jnp.int32), shape((rows, nodes), BF16)),
        [HBM, HBM],
        (VMEM, VMEM),
        scratch=[pltpu.SMEM((1, peers), jnp.int32), dma((2,))],
    )(halo_block, features)
    asked = swap(request, "dom")
    outgoing = call(
        pack_kernel,
        shape((peers, rows, lanes), BF16),
        [VMEM, VMEM],
        HBM,
        scratch=[pltpu.VMEM((peers, rows, lanes), BF16), dma((4,))],
    )(asked, near)
    incoming = swap(outgoing, "dom")
    cotangent, _ = lax.optimization_barrier((cotangent, asked))
    cot_full = lax.all_gather(cotangent, "feat", axis=0, tiled=True)

    spread = forward(tile_src, tile_dst, tile_count, near, incoming, tile_vals, cot_full)
    agg = swap(spread, "feat")

    part, pre_grad, activated = call(
        middle_kernel,
        (shape((GROUP, EXTRA, lanes), F32), shape((full, nodes), BF16), shape((rows, nodes), BF16)),
        [VMEM, VMEM, VMEM],
        (VMEM, VMEM, VMEM),
        scratch=[pltpu.VMEM((full, nodes), F32)],
    )(agg, weight, cot_full)

    groups = [
        [(2 * a + i) * 8 + 4 * b + j for i in range(2) for j in range(4)]
        for a in range(peers // 16)
        for b in range(2)
    ]
    parts = swap(part, "dom", axis_index_groups=groups)

    outbound, own = backward(
        tile_src, tile_dst, tile_count, pre_grad, weight, tile_vals, rows, peers
    )
    outbound = call(
        attach_kernel, shape((peers, rows + EXTRA, lanes), BF16), [VMEM, VMEM], aliases={1: 0}
    )(parts, outbound)
    returned = swap(outbound, "dom")

    feature_grad, weight_grad = call(
        functools.partial(final_kernel, 1.0 / math.sqrt(peers * nodes)),
        (shape((rows, nodes), BF16), shape((rows, full), F32)),
        [VMEM, HBM, VMEM],
        (VMEM, VMEM),
        scratch=[pltpu.VMEM((blocks, rows, lanes), F32), dma(())],
    )(asked, own, returned)
    return (activated, feature_grad, weight_grad)


def solution(mesh):
    return jax.shard_map(
        shards,
        mesh=mesh,
        in_specs=(
            P("feat", "dom"),
            P(),
            P("feat", "dom"),
            P("dom", None, None),
            P("dom"),
            P("dom"),
            P("dom"),
            P("dom", None),
        ),
        out_specs=(P("feat", "dom"), P("feat", "dom"), P("feat", None)),
        check_vma=False,
    )
```

```python
import functools
import math

import jax
import jax.numpy as jnp
from jax import lax
from jax.experimental import pallas as pl
from jax.experimental.pallas import tpu as pltpu
from jax.sharding import PartitionSpec as P

BF16, F32 = jnp.bfloat16, jnp.float32
VMEM = pl.BlockSpec(memory_space=pltpu.VMEM)
HBM = pl.BlockSpec(memory_space=pltpu.HBM)
ANY = pl.BlockSpec(memory_space=pl.ANY)
CHUNK = 35
GROUP = 8
EXTRA = 8


def call(kernel, out_shape, in_specs, out_specs=None, scratch=(), flops=1000, nbytes=1000, aliases=None):
    return pl.pallas_call(
        kernel,
        out_shape=out_shape,
        in_specs=in_specs,
        out_specs=VMEM if out_specs is None else out_specs,
        scratch_shapes=list(scratch),
        input_output_aliases=aliases or {},
        cost_estimate=pl.CostEstimate(flops=flops, bytes_accessed=nbytes, transcendentals=0),
        compiler_params=pltpu.CompilerParams(vmem_limit_bytes=24 * 1024 * 1024),
    )


def request_kernel(halo_hbm, feat_hbm, out_ref, feat_ref, halo_ref, sems):
    first = pltpu.make_async_copy(halo_hbm, halo_ref, sems.at[0])
    second = pltpu.make_async_copy(feat_hbm, feat_ref, sems.at[1])
    first.start()
    second.start()
    first.wait()
    for q in range(out_ref.shape[0]):
        out_ref[q] = jnp.full((1, out_ref.shape[2]), halo_ref[0, q], jnp.int32)
    second.wait()


def pack_kernel(asked_ref, feat_ref, out_hbm, out_ref, sems):
    peers, rows, lanes = out_ref.shape
    step = peers // sems.shape[0]
    copies = [
        pltpu.make_async_copy(
            out_ref.at[pl.ds(i * step, step)], out_hbm.at[pl.ds(i * step, step)], sems.at[i]
        )
        for i in range(sems.shape[0])
    ]
    blocks = feat_ref.shape[1] // lanes
    own = [
        feat_ref[:, b * lanes : (b + 1) * lanes].astype(F32).reshape(rows // 8, 8, lanes)
        for b in range(blocks)
    ]
    for q in range(peers):
        want = jnp.broadcast_to(asked_ref[q], (8, lanes))
        piece = own[0]
        for b in range(1, blocks):
            piece = jnp.where((want == b)[None], own[b], piece)
        out_ref[q] = piece.reshape(rows, lanes).astype(BF16)
        if q % step == step - 1:
            copies[q // step].start()
    for copy in copies:
        copy.wait()


def tile_copies(tiles_hbm, tiles_ref, sems):
    return [
        pltpu.make_async_copy(
            tiles_hbm.at[pl.ds(c * CHUNK, CHUNK)], tiles_ref.at[pl.ds(c * CHUNK, CHUNK)], sems.at[c]
        )
        for c in range(tiles_ref.shape[0] // CHUNK)
    ]


def forward_kernel(
    src_hbm, dst_hbm, count_hbm, near_ref, halo_ref, tiles_hbm, _,
    out_ref, acc_ref, table_ref, tiles_ref, src_ref, dst_ref, count_ref, small_sems, sems,
):
    tile_total, lanes, _ = tiles_ref.shape
    blocks = near_ref.shape[1] // lanes
    small = [
        pltpu.make_async_copy(a, b, small_sems.at[i])
        for i, (a, b) in enumerate(((src_hbm, src_ref), (dst_hbm, dst_ref), (count_hbm, count_ref)))
    ]
    big = tile_copies(tiles_hbm, tiles_ref, sems)
    for copy in small + big:
        copy.start()
    acc_ref[...] = jnp.zeros_like(acc_ref)
    for b in range(blocks):
        table_ref[b] = near_ref[:, b * lanes : (b + 1) * lanes]
    table_ref[blocks:] = halo_ref[...]
    for copy in small:
        copy.wait()
    count = count_ref[0]

    def chunk(c):
        terms = []
        for t in range(c * CHUNK, (c + 1) * CHUNK):
            terms.append(
                lax.dot_general(
                    table_ref[src_ref[t]],
                    tiles_ref[t],
                    (((1,), (1,)), ((), ())),
                    preferred_element_type=F32,
                )
            )
        for i, t in enumerate(range(c * CHUNK, (c + 1) * CHUNK)):
            acc_ref[jnp.where(t < count, dst_ref[t], blocks)] += terms[i]

    for c in range(tile_total // CHUNK):
        big[c].wait()
        pl.when(c * CHUNK < count)(functools.partial(chunk, c))

    for b in range(blocks):
        block = acc_ref[b].astype(BF16)
        for e in range(out_ref.shape[0]):
            out_ref[e, :, b * lanes : (b + 1) * lanes] = block


def forward(src, dst, count, near, halo, tiles, cot_full):
    rows, nodes = near.shape
    total, lanes, _ = tiles.shape
    blocks = nodes // lanes
    dma = pltpu.SemaphoreType.DMA
    return call(
        forward_kernel,
        jax.ShapeDtypeStruct((cot_full.shape[0] // rows, rows, nodes), BF16),
        [HBM, HBM, HBM, VMEM, VMEM, HBM, ANY],
        scratch=[
            pltpu.VMEM((blocks + 1, rows, lanes), F32),
            pltpu.VMEM((blocks + halo.shape[0], rows, lanes), BF16),
            pltpu.VMEM((total, lanes, lanes), BF16),
            pltpu.SMEM((total,), jnp.int32),
            pltpu.SMEM((total,), jnp.int32),
            pltpu.SMEM((1,), jnp.int32),
            dma((3,)),
            dma((total // CHUNK,)),
        ],
    )(src, dst, count, near, halo, tiles, cot_full)


def middle_kernel(agg_ref, weight_ref, cot_ref, part_ref, pre_grad_ref):
    feats, rows, nodes = agg_ref.shape
    lanes = part_ref.shape[2]
    index = lax.axis_index("feat")
    agg = agg_ref[...].reshape(feats * rows, nodes)
    pre = lax.dot_general(
        weight_ref[...], agg, (((0,), (0,)), ((), ())), preferred_element_type=F32
    )
    sig = jax.nn.sigmoid(pre)
    grad = (cot_ref[...].astype(F32) * sig * (1.0 + pre * (1.0 - sig))).astype(BF16)
    part = lax.dot_general(
        agg_ref[index], grad, (((1,), (1,)), ((), ())), preferred_element_type=F32
    )
    height = rows // GROUP
    for r in range(GROUP):
        part_ref[r] = jnp.concatenate(
            [
                part[r * height : (r + 1) * height, i * lanes : (i + 1) * lanes]
                for i in range(part.shape[1] // lanes)
            ],
            axis=0,
        )
    pre_grad_ref[...] = grad


def backward_kernel(
    src_hbm, dst_hbm, count_hbm, pre_grad_ref, weight_ref, agg_ref, tiles_hbm,
    out_ref, own_hbm, act_ref, acc_ref, grad_ref, pre_ref, tiles_ref, src_ref, dst_ref, count_ref, small_sems, sems,
):
    rows, nodes = grad_ref.shape
    tile_total, lanes, _ = tiles_ref.shape
    blocks = grad_ref.shape[1] // lanes
    spare = acc_ref.shape[0] - 1
    small = [
        pltpu.make_async_copy(a, b, small_sems.at[i])
        for i, (a, b) in enumerate(((src_hbm, src_ref), (dst_hbm, dst_ref), (count_hbm, count_ref)))
    ]
    big = tile_copies(tiles_hbm, tiles_ref, sems)
    for copy in small + big:
        copy.start()
    mine = pl.ds(pl.multiple_of(lax.axis_index("feat") * rows, rows), rows)
    grad_ref[...] = jnp.dot(
        weight_ref[mine, :], pre_grad_ref[...], preferred_element_type=F32
    ).astype(BF16)
    acc_ref[...] = jnp.zeros_like(acc_ref)
    for copy in small:
        copy.wait()
    count = count_ref[0]

    def chunk(c):
        terms = []
        for t in range(c * CHUNK, (c + 1) * CHUNK):
            start = pl.multiple_of(dst_ref[t] * lanes, lanes)
            terms.append(
                jnp.dot(grad_ref[:, pl.ds(start, lanes)], tiles_ref[t], preferred_element_type=F32)
            )
        for i, t in enumerate(range(c * CHUNK, (c + 1) * CHUNK)):
            acc_ref[jnp.where(t < count, src_ref[t], spare)] += terms[i]

    for c in range(tile_total // CHUNK):
        big[c].wait()
        pl.when(c * CHUNK < count)(functools.partial(chunk, c))

    keep = pltpu.make_async_copy(acc_ref.at[pl.ds(0, blocks)], own_hbm, small_sems.at[3])
    keep.start()
    for q in range(out_ref.shape[0]):
        out_ref[q, :rows, :] = acc_ref[blocks + q].astype(BF16)
    pre_ref[...] = lax.dot_general(
        weight_ref[...],
        agg_ref[...].reshape(-1, nodes),
        (((0,), (0,)), ((), ())),
        preferred_element_type=F32,
    )
    act_ref[...] = jax.nn.silu(pre_ref[mine, :]).astype(BF16)
    keep.wait()


def backward(src, dst, count, pre_grad, weight, agg, tiles, peers):
    _, rows, nodes = agg.shape
    total, lanes, _ = tiles.shape
    blocks = nodes // lanes
    dma = pltpu.SemaphoreType.DMA
    return call(
        backward_kernel,
        (
            jax.ShapeDtypeStruct((peers, rows + EXTRA, lanes), BF16),
            jax.ShapeDtypeStruct((blocks, rows, lanes), F32),
            jax.ShapeDtypeStruct((rows, nodes), BF16),
        ),
        [HBM, HBM, HBM, VMEM, VMEM, VMEM, HBM],
        (VMEM, HBM, VMEM),
        scratch=[
            pltpu.VMEM((blocks + peers + 1, rows, lanes), F32),
            pltpu.VMEM((rows, nodes), BF16),
            pltpu.VMEM(pre_grad.shape, F32),
            pltpu.VMEM((total, lanes, lanes), BF16),
            pltpu.SMEM((total,), jnp.int32),
            pltpu.SMEM((total,), jnp.int32),
            pltpu.SMEM((1,), jnp.int32),
            dma((4,)),
            dma((total // CHUNK,)),
        ],
        flops=200_000_000,
        nbytes=20_000_000,
    )(src, dst, count, pre_grad, weight, agg, tiles)


def attach_kernel(parts_ref, _, out_ref):
    rows = out_ref.shape[1] - EXTRA
    total = parts_ref[0]
    for i in range(1, parts_ref.shape[0]):
        total = total + parts_ref[i]
    total = total.astype(BF16)
    for q in range(out_ref.shape[0]):
        out_ref[q, rows:, :] = total


def final_kernel(scale, asked_ref, own_hbm, back_ref, grad_ref, weight_ref, own_ref, sem):
    blocks, rows, lanes = own_ref.shape
    peers = back_ref.shape[0]
    fetch = pltpu.make_async_copy(own_hbm, own_ref, sem)
    fetch.start()
    sums = [jnp.zeros((rows // 8, 8, lanes), F32)] * blocks
    pieces = [None] * GROUP
    for q in range(peers):
        want = jnp.broadcast_to(asked_ref[q], (8, lanes))
        term = back_ref[q, :rows, :].astype(F32).reshape(rows // 8, 8, lanes)
        for b in range(blocks):
            sums[b] = sums[b] + jnp.where((want == b)[None], term, 0.0)
        r = (q // 8 % 2) * 4 + q % 4
        piece = back_ref[q, rows:, :].astype(F32)
        pieces[r] = piece if pieces[r] is None else pieces[r] + piece
    height = rows // GROUP
    for r in range(GROUP):
        for i in range(EXTRA // height):
            weight_ref[r * height : (r + 1) * height, i * lanes : (i + 1) * lanes] = (
                pieces[r][i * height : (i + 1) * height] * scale
            )
    fetch.wait()
    for b in range(blocks):
        grad_ref[:, b * lanes : (b + 1) * lanes] = (
            sums[b].reshape(rows, lanes) + own_ref[b]
        ).astype(BF16)


def shards(features, weight, cotangent, tile_vals, tile_src, tile_dst, tile_count, halo_block):
    rows, nodes = features.shape
    lanes = tile_vals.shape[2]
    blocks = nodes // lanes
    peers = lax.axis_size("dom")
    feats = lax.axis_size("feat")
    full = rows * feats
    shape = jax.ShapeDtypeStruct
    swap = functools.partial(lax.all_to_all, split_axis=0, concat_axis=0, tiled=True)
    dma = pltpu.SemaphoreType.DMA
    held = functools.partial(pltpu.with_memory_space_constraint, memory_space=pltpu.HBM)
    features, tile_vals, halo_block = held(features), held(tile_vals), held(halo_block)
    tile_src, tile_dst = held(tile_src), held(tile_dst)

    request, near = call(
        request_kernel,
        (shape((peers, 1, lanes), jnp.int32), shape((rows, nodes), BF16)),
        [HBM, HBM],
        (VMEM, VMEM),
        scratch=[pltpu.SMEM((1, peers), jnp.int32), dma((2,))],
    )(halo_block, features)
    asked = swap(request, "dom")
    outgoing = call(
        pack_kernel,
        shape((peers, rows, lanes), BF16),
        [VMEM, VMEM],
        HBM,
        scratch=[pltpu.VMEM((peers, rows, lanes), BF16), dma((4,))],
    )(asked, near)
    incoming = swap(outgoing, "dom")
    cotangent, _ = lax.optimization_barrier((cotangent, asked))
    cot_full = lax.all_gather(cotangent, "feat", axis=0, tiled=True)

    spread = forward(tile_src, tile_dst, tile_count, near, incoming, tile_vals, cot_full)
    agg = swap(spread, "feat")

    part, pre_grad = call(
        middle_kernel,
        (shape((GROUP, EXTRA, lanes), F32), shape((full, nodes), BF16)),
        [VMEM, VMEM, VMEM],
        (VMEM, VMEM),
    )(agg, weight, cot_full)

    groups = [
        [(2 * a + i) * 8 + 4 * b + j for i in range(2) for j in range(4)]
        for a in range(peers // 16)
        for b in range(2)
    ]
    parts = swap(part, "dom", axis_index_groups=groups)

    outbound, own, activated = backward(
        tile_src, tile_dst, tile_count, pre_grad, weight, agg, tile_vals, peers
    )
    outbound = call(
        attach_kernel, shape((peers, rows + EXTRA, lanes), BF16), [VMEM, VMEM], aliases={1: 0}
    )(parts, outbound)
    returned = swap(outbound, "dom")

    feature_grad, weight_grad = call(
        functools.partial(final_kernel, 1.0 / math.sqrt(peers * nodes)),
        (shape((rows, nodes), BF16), shape((rows, full), F32)),
        [VMEM, HBM, VMEM],
        (VMEM, VMEM),
        scratch=[pltpu.VMEM((blocks, rows, lanes), F32), dma(())],
    )(asked, own, returned)
    return (activated, feature_grad, weight_grad)


def solution(mesh):
    return jax.shard_map(
        shards,
        mesh=mesh,
        in_specs=(
            P("feat", "dom"),
            P(),
            P("feat", "dom"),
            P("dom", None, None),
            P("dom"),
            P("dom"),
            P("dom"),
            P("dom", None),
        ),
        out_specs=(P("feat", "dom"), P("feat", "dom"), P("feat", None)),
        check_vma=False,
    )
```
